32 devices in a mesh: tm: 4 (over y, x), space: 8 (over z, core).
Axes of the slice: x: 2, y: 2, z: 4, core: 2. Of those that a mesh axis runs over, the one named last changes fastest.
Arguments:
- starts: float32 [4, 8, 32, 128, 128], P('tm', None, 'space'), may hold values from -6 to 6
- classes: int32 [32, 128, 128], P('space'), may hold values from 0 to 15
- dispersion_table: float32 [16, 8], replicated, may hold values from 0.0015 to 0.015
- mixing: float32 [8, 8], replicated, may hold values from -0.04 to 1, as said below
Outputs:
- slice_ends: float32 [4, 8, 32, 128, 128], P('tm', None, 'space')
The draws below stay inside these ranges and needn't reach their ends.
Inputs may be any that keep to these rules, and one draw needn't show every extreme that they name: mixing has 1 minus a positive decay rate of at most 0.3 on its diagonal, and off-diagonal couplings between -0.04 and 0.04.
All inputs are finite; a program needn't handle non-finite values.
Results may differ from the reference program's by a relative error of at most 0.00013.
Values sent between devices are 32-bit elements; how exact they have to be, the bound alone decides.
A program may use at most 128 MiB of HBM per device.

```python
import math
import jax
import jax.numpy as jnp
from jax import lax

SPECIES = 8
CLASSES = 16
NY = 128
NZ = 128
SLICES = 4
NX = 32


def draw_mixing(key, part):
    first_key = jax.random.fold_in(key, 11)
    second_key = jax.random.fold_in(key, 23)
    decay_rates = jnp.exp(jax.random.uniform(first_key, (SPECIES,), jnp.float32, math.log(0.01), math.log(0.3)))
    coupling = jax.random.uniform(second_key, (SPECIES, SPECIES), jnp.float32, -0.04, 0.04)
    identity = jnp.eye(SPECIES, dtype=jnp.float32)
    return identity * (1.0 - decay_rates)[:, None] + (1.0 - identity) * coupling


def touch_ends(drawn, stream_key, low, largest):
    shape = drawn.shape
    place = [jax.random.randint(jax.random.fold_in(stream_key, axis), (), 0, shape[axis]) for axis in range(len(shape))]
    drawn = drawn.at[tuple(place)].set(low)
    longest = shape.index(max(shape))
    place[longest] = (place[longest] + 1) % shape[longest]
    return drawn.at[tuple(place)].set(largest)


def shard_levels(stream_key, shape, cuts, least, largest):
    gain = 1.0
    for dim, shards_of in cuts:
        steps = jax.random.uniform(jax.random.fold_in(jax.random.fold_in(stream_key, 6), dim), (shards_of,), jnp.float32, least / len(cuts), largest / len(cuts))
        gain = gain * jnp.repeat(jnp.exp(steps), shape[dim] // shards_of).reshape((-1,) + (1,) * (len(shape) - 1 - dim))
    return gain


def bell_draw(key, shape, spread, reach, cuts=(), kind=jnp.bfloat16):
    result = spread * jax.random.normal(key, shape, jnp.float32)
    if cuts:
        result = result * shard_levels(key, shape, cuts, -0.22, 0.18)
    return jnp.clip(result, -reach, reach).astype(kind)


def setup_inputs(seed: int = 0) -> dict:
    seeds = jax.random.split(jax.random.key(seed), 5)
    starts = bell_draw(seeds[0], (SLICES, SPECIES, NX, NY, NZ), 1.0, 6.0, ((0, 4), (2, 8)), jnp.float32)
    classes = touch_ends(jax.random.randint(seeds[1], (NX, NY, NZ), 0, CLASSES), jax.random.fold_in(seeds[1], 1), 0, CLASSES - 1).astype(jnp.int32)
    dispersion_table = jnp.clip(jnp.exp(jax.random.uniform(seeds[2], (CLASSES, SPECIES), jnp.float32, math.log(0.0015), math.log(0.015))), 0.0015, 0.015)
    mixing = draw_mixing(jax.random.fold_in(seeds[4], 71), 0)
    return dict(starts=starts, classes=classes, dispersion_table=dispersion_table, mixing=mixing)


corner_weights = (1.0, 0.5, 0.25)
fine_courant = (0.15, 0.1, 0.05)
coarse_courant = (0.3, 0.2, 0.1)


def advance(padded, kappa, coarse_form):
    extent_x = padded.shape[1] - 2
    extent_y = padded.shape[2] - 2
    extent_z = padded.shape[3] - 2
    centre = padded[:, 1:1 + extent_x, 1:1 + extent_y, 1:1 + extent_z]
    kappa_here = kappa[:, 1:1 + extent_x, 1:1 + extent_y, 1:1 + extent_z]
    summed = jnp.zeros_like(centre)
    for shift_x in (-1, 0, 1):
        for shift_y in (-1, 0, 1):
            for shift_z in (-1, 0, 1):
                order_level = abs(shift_x) + abs(shift_y) + abs(shift_z)
                if order_level == 0:
                    continue
                if coarse_form and order_level > 1:
                    continue
                weight = 2.0 if coarse_form else 0.5 * corner_weights[order_level - 1]
                neighbour = padded[:, 1 + shift_x:1 + shift_x + extent_x, 1 + shift_y:1 + shift_y + extent_y, 1 + shift_z:1 + shift_z + extent_z]
                kappa_near = kappa[:, 1 + shift_x:1 + shift_x + extent_x, 1 + shift_y:1 + shift_y + extent_y, 1 + shift_z:1 + shift_z + extent_z]
                summed = summed + weight * (kappa_here + kappa_near) * (neighbour - centre)
    courant = coarse_courant if coarse_form else fine_courant
    upwind = courant[0] * (centre - padded[:, 0:extent_x, 1:1 + extent_y, 1:1 + extent_z])
    upwind = upwind + courant[1] * (centre - padded[:, 1:1 + extent_x, 0:extent_y, 1:1 + extent_z])
    upwind = upwind + courant[2] * (centre - padded[:, 1:1 + extent_x, 1:1 + extent_y, 0:extent_z])
    return centre + summed - upwind


def species_mix(mixing, moved):
    return jnp.einsum('st,txyz->sxyz', mixing, moved, precision=lax.Precision.HIGHEST)


def pad_space(field):
    return jnp.pad(field, ((0, 0), (1, 1), (1, 1), (1, 1)))


def reference(starts, classes, dispersion_table, mixing):
    class_padded = jnp.pad(classes, 1)
    kappa = jnp.moveaxis(dispersion_table[class_padded], -1, 0)

    def fine(field):
        for repeat in range(2):
            field = species_mix(mixing, advance(pad_space(field), kappa, False))
        return field

    def coarse(field):
        return species_mix(mixing, advance(pad_space(field), kappa, True))

    collected = []
    current_end = starts[0]
    for position in range(starts.shape[0]):
        correction = fine(starts[position]) - coarse(starts[position])
        current_end = coarse(current_end) + correction
        collected.append(current_end)
    return jnp.stack(collected)
```

```python
import functools

import jax
import jax.numpy as jnp
from jax import lax
from jax.experimental import pallas as pl
from jax.experimental.pallas import tpu as pltpu
from jax.sharding import PartitionSpec as P

ROWS = 8
PAD = 8
fine_courant = (0.15, 0.1, 0.05)
coarse_courant = (0.3, 0.2, 0.1)


def kernel(
    TM, SP, table, mixing, starts, classes, out,
    u0, u1, w, kq, ef, ec, cl, moved,
    local_sem, cls_send, cls_recv, h0_send, h0_recv, h1_send, h1_recv,
    wh_send, wh_recv, w_send, w_recv,
):
    S, X, Y, Z = out.shape
    C = table.shape[0]
    NC = Y // ROWS
    NG = h0_send.shape[1]
    group_rows = Y // NG
    per_group = group_rows // ROWS
    tm = lax.axis_index("tm")
    sp = lax.axis_index("space")
    has_up = sp < SP - 1
    has_down = sp > 0
    has_next = tm < TM - 1
    has_prev = tm > 0

    def rows(c):
        return pl.ds(pl.multiple_of(c * ROWS, ROWS), ROWS)

    def padded_rows(c):
        return pl.ds(pl.multiple_of(c * ROWS + PAD, ROWS), ROWS)

    def remote(src, dst, send, recv, **device):
        return pltpu.make_async_remote_copy(
            src_ref=src, dst_ref=dst, send_sem=send, recv_sem=recv,
            device_id=device, device_id_type=pl.DeviceIdType.MESH,
        )

    def cls_copy(k):
        edge = X - 1 if k == 0 else 0
        place = 0 if k == 0 else X + 1
        to = sp + 1 if k == 0 else sp - 1
        return remote(classes.at[edge], cl.at[place], cls_send.at[k], cls_recv.at[k], space=to)

    def h0_copy(k, g):
        edge = X - 1 if k == 0 else 0
        place = 0 if k == 0 else X + 1
        to = sp + 1 if k == 0 else sp - 1
        src = starts.at[0, :, edge, pl.ds(pl.multiple_of(g * group_rows, ROWS), group_rows), :]
        dst = u0.at[:, place, pl.ds(pl.multiple_of(g * group_rows + PAD, ROWS), group_rows), :]
        return remote(src, dst, h0_send.at[k, g], h0_recv.at[k, g], space=to)

    def halo_copy(field, send, recv, k, c):
        edge = X if k == 0 else 1
        place = 0 if k == 0 else X + 1
        to = sp + 1 if k == 0 else sp - 1
        return remote(
            field.at[:, edge, padded_rows(c), :], field.at[:, place, padded_rows(c), :],
            send.at[k, c], recv.at[k, c], space=to,
        )

    h1_copy = functools.partial(halo_copy, u1, h1_send, h1_recv)
    wh_copy = functools.partial(halo_copy, w, wh_send, wh_recv)

    def w_copy(c):
        return remote(
            out.at[:, :, rows(c), :], w.at[:, pl.ds(1, X), padded_rows(c), :],
            w_send.at[c], w_recv.at[c], tm=tm + 1,
        )

    def start_both(copy, *args):
        pl.when(has_up)(lambda: copy(0, *args).start())
        pl.when(has_down)(lambda: copy(1, *args).start())

    def recv_both(copy, *args):
        pl.when(has_down)(lambda: copy(0, *args).wait_recv())
        pl.when(has_up)(lambda: copy(1, *args).wait_recv())

    def sent_both(copy, *args):
        pl.when(has_up)(lambda: copy(0, *args).wait_send())
        pl.when(has_down)(lambda: copy(1, *args).wait_send())

    start_in = pltpu.make_async_copy(
        starts.at[0], u0.at[:, pl.ds(1, X), pl.ds(PAD, Y), :], local_sem.at[0]
    )
    class_in = pltpu.make_async_copy(classes, cl.at[pl.ds(1, X)], local_sem.at[1])
    start_in.start()
    class_in.start()

    barrier = pltpu.get_barrier_semaphore()
    for exists, device in (
        (has_up, dict(space=sp + 1)), (has_down, dict(space=sp - 1)),
        (has_next, dict(tm=tm + 1)), (has_prev, dict(tm=tm - 1)),
    ):
        def greet(device=device):
            pl.semaphore_signal(
                barrier, inc=1, device_id=device, device_id_type=pl.DeviceIdType.MESH
            )
        pl.when(exists)(greet)

    tile_all = jnp.zeros((X + 2, PAD, Z), jnp.float32)

    def clear(s, carry):
        for field in (u0, u1, w):
            field[s, :, 0:PAD, :] = tile_all
            field[s, :, Y + PAD : Y + 2 * PAD, :] = tile_all
        outside = jnp.full((X + 2, PAD, Z), table[0, s] * 0.125, jnp.float32)
        kq[s, :, 0:PAD, :] = outside
        kq[s, :, Y + PAD : Y + 2 * PAD, :] = outside
        return carry

    lax.fori_loop(0, S, clear, 0)

    def clear_plane(place):
        def one(s, carry):
            for field in (u0, u1, w):
                field[s, place, PAD : Y + PAD, :] = jnp.zeros((Y, Z), jnp.float32)
            return carry
        lax.fori_loop(0, S, one, 0)
        cl[place] = jnp.zeros((Y, Z), jnp.int32)

    pl.when(jnp.logical_not(has_down))(lambda: clear_plane(0))
    pl.when(jnp.logical_not(has_up))(lambda: clear_plane(X + 1))

    neighbours = (
        has_up.astype(jnp.int32) + has_down.astype(jnp.int32)
        + has_next.astype(jnp.int32) + has_prev.astype(jnp.int32)
    )
    pl.semaphore_wait(barrier, neighbours)

    start_both(cls_copy)
    for g in range(NG):
        start_both(h0_copy, g)
    start_in.wait()
    class_in.wait()
    recv_both(cls_copy)

    lane = lax.broadcasted_iota(jnp.int32, (X, ROWS, Z), 2)
    at_first = lane == 0
    at_last = lane == Z - 1

    def behind(value, fill=0.0):
        return jnp.where(at_first, fill, pltpu.roll(value, 1, 2))

    def ahead(value, fill=0.0):
        return jnp.where(at_last, fill, pltpu.roll(value, Z - 1, 2))

    def three(field, s, c, inner):
        base = c * ROWS + PAD
        planes = pl.ds(1, X) if inner else slice(None)
        before = field[s, planes, pl.ds(base - 1, ROWS), :]
        here = field[s, :, padded_rows(c), :]
        after = field[s, planes, pl.ds(base + 1, ROWS), :]
        return before, here, after

    def smooth_x(value):
        middle = value[1:-1]
        return (value[:-2] + value[2:]) + (middle + middle)

    def kappa(c):
        found = cl[:, rows(c), :]
        bits = []
        level = 1
        while level < C:
            bits.append((found & level) != 0)
            level *= 2

        def one(s, carry):
            values = [table[i, s] for i in range(C)]
            for bit in bits:
                values = [
                    jnp.where(bit, values[i + 1], values[i]) if i + 1 < len(values) else values[i]
                    for i in range(0, len(values), 2)
                ]
            kq[s, :, padded_rows(c), :] = jnp.broadcast_to(values[0], found.shape) * 0.125
            return carry

        lax.fori_loop(0, S, one, 0)

    def coefficients(c):
        def one(s, carry):
            before, here, after = three(kq, s, c, False)
            outside = table[0, s] * 0.125
            mid = here[1:-1]
            smooth = smooth_x((before + after) + (here + here))
            smooth = (smooth + smooth) + (
                behind(smooth, outside * 16.0) + ahead(smooth, outside * 16.0)
            )
            ef[s, :, rows(c), :] = (1.0 - sum(fine_courant)) - 64.0 * mid - smooth
            faces = (here[:-2] + here[2:]) + (before[1:-1] + after[1:-1])
            faces = faces + (behind(mid, outside) + ahead(mid, outside))
            ec[s, :, rows(c), :] = (1.0 - sum(coarse_courant)) - 96.0 * mid - 16.0 * faces
            return carry

        lax.fori_loop(0, S, one, 0)

    def fine_move(field, s, c):
        before, here, after = three(field, s, c, False)
        k_before, k_here, k_after = three(kq, s, c, False)
        product = k_here * here
        weighted = (k_before * before + k_after * after) + (product + product)
        plain = smooth_x((before + after) + (here + here))
        weighted = smooth_x(weighted)
        mid = here[1:-1]
        result = mid * ef[s, :, rows(c), :]
        result += fine_courant[0] * here[:-2] + fine_courant[1] * before[1:-1]
        result += k_here[1:-1] * ((plain + plain) + (behind(plain) + ahead(plain)))
        result += (weighted + weighted) + (
            behind(weighted + fine_courant[2] * mid) + ahead(weighted)
        )
        return result

    def coarse_move(field, s, c):
        before, here, after = three(field, s, c, True)
        k_before, k_here, k_after = three(kq, s, c, True)
        mid = here[1:-1]
        k_mid = k_here[1:-1]
        product = k_here * here
        mid_product = product[1:-1]
        plain = (here[:-2] + here[2:]) + (before + after)
        plain = plain + (behind(mid) + ahead(mid))
        weighted = (product[:-2] + product[2:]) + (k_before * before + k_after * after)
        weighted = weighted + (
            behind(mid_product + (coarse_courant[2] / 16.0) * mid) + ahead(mid_product)
        )
        result = mid * ec[s, :, rows(c), :]
        result += coarse_courant[0] * here[:-2] + coarse_courant[1] * before
        return result + 16.0 * (k_mid * plain + weighted)

    def mix(store):
        values = [moved[t] for t in range(S)]
        for s in range(S):
            total = mixing[s, 0] * values[0]
            for t in range(1, S):
                total += mixing[s, t] * values[t]
            store(s, total)

    def each_species(move):
        def one(s, carry):
            moved[s] = move(s)
            return carry
        lax.fori_loop(0, S, one, 0)

    def first_fine(c):
        each_species(lambda s: fine_move(u0, s, c))

        def store(s, value):
            u1[s, 1 : X + 1, padded_rows(c), :] = value

        mix(store)
        start_both(h1_copy, c)

    def store_out(c):
        def store(s, value):
            out[s, :, rows(c), :] = value
        return store

    def second_fine(c):
        @pl.when(jnp.logical_not(has_prev))
        def _():
            each_species(lambda s: fine_move(u1, s, c))
            mix(store_out(c))
            pl.when(has_next)(lambda: w_copy(c).start())

        @pl.when(has_prev)
        def _():
            each_species(lambda s: fine_move(u1, s, c) - coarse_move(u0, s, c))
            mix(store_out(c))

    def own_step(t, carry):
        @pl.when(t < NC)
        def _():
            pl.when(lax.rem(t, per_group) == 0)(lambda: recv_both(h0_copy, t // per_group))
            kappa(t)

        @pl.when(jnp.logical_and(t >= 1, t <= NC))
        def _():
            coefficients(t - 1)
            first_fine(t - 1)

        @pl.when(jnp.logical_and(t >= 2, t <= NC + 1))
        def _():
            recv_both(h1_copy, t - 2)

        pl.when(t >= 3)(lambda: second_fine(t - 3))
        return carry

    lax.fori_loop(0, NC + 3, own_step, 0)

    def chain_step(t, carry):
        @pl.when(t < NC)
        def _():
            w_copy(t).wait_recv()
            start_both(wh_copy, t)

        @pl.when(t >= 1)
        def _():
            c = t - 1
            recv_both(wh_copy, c)
            each_species(lambda s: coarse_move(w, s, c))

            def store(s, value):
                out[s, :, rows(c), :] = out[s, :, rows(c), :] + value

            mix(store)
            pl.when(has_next)(lambda: w_copy(c).start())
        return carry

    @pl.when(has_prev)
    def _():
        lax.fori_loop(0, NC + 1, chain_step, 0)

    sent_both(cls_copy)
    for g in range(NG):
        sent_both(h0_copy, g)

    def finish(c, carry):
        sent_both(h1_copy, c)
        pl.when(has_prev)(lambda: sent_both(wh_copy, c))
        pl.when(has_next)(lambda: w_copy(c).wait_send())
        return carry

    lax.fori_loop(0, NC, finish, 0)


def solution(mesh):
    TM, SP = mesh.shape["tm"], mesh.shape["space"]

    def body(starts, classes, table, mixing):
        _, S, X, Y, Z = starts.shape
        NC = Y // ROWS
        NG = 4
        padded = pltpu.VMEM((S, X + 2, Y + 2 * PAD, Z), jnp.float32)
        plain = pltpu.VMEM((S, X, Y, Z), jnp.float32)
        dma = pltpu.SemaphoreType.DMA
        result = pl.pallas_call(
            functools.partial(kernel, TM, SP),
            out_shape=jax.ShapeDtypeStruct((S, X, Y, Z), jnp.float32),
            in_specs=[
                pl.BlockSpec(memory_space=pltpu.SMEM),
                pl.BlockSpec(memory_space=pltpu.SMEM),
                pl.BlockSpec(memory_space=pl.ANY),
                pl.BlockSpec(memory_space=pl.ANY),
            ],
            out_specs=pl.BlockSpec(memory_space=pltpu.VMEM),
            scratch_shapes=[
                padded, padded, padded, padded, plain, plain,
                pltpu.VMEM((X + 2, Y, Z), jnp.int32),
                pltpu.VMEM((S, X, ROWS, Z), jnp.float32),
                dma((2,)), dma((2,)), dma((2,)), dma((2, NG)), dma((2, NG)),
                dma((2, NC)), dma((2, NC)), dma((2, NC)), dma((2, NC)),
                dma((NC,)), dma((NC,)),
            ],
            compiler_params=pltpu.CompilerParams(
                collective_id=0, has_side_effects=True, vmem_limit_bytes=48 * 1024 * 1024
            ),
        )(table, mixing, starts, classes)
        return result[None]

    in_specs = (P("tm", None, "space", None, None), P("space", None, None), P(), P())
    out_specs = P("tm", None, "space", None, None)
    return jax.shard_map(body, mesh=mesh, in_specs=in_specs, out_specs=out_specs, check_vma=False)
```

```python
import functools

import jax
import jax.numpy as jnp
from jax import lax
from jax.experimental import pallas as pl
from jax.experimental.pallas import tpu as pltpu
from jax.sharding import PartitionSpec as P

ROWS = 8
BEHIND = 4
LAG = 2
LAG0 = 0
UNROLL = 4
PAD = 8
fine_courant = (0.15, 0.1, 0.05)
coarse_courant = (0.3, 0.2, 0.1)


def kernel(
    TM, SP, table, mixing, starts, classes, out,
    u0, u1, w, kq, ef, ec, cl, moved,
    local_sem, cls_send, cls_recv, h0_send, h0_recv, h1_send, h1_recv,
    wh_send, wh_recv, w_send, w_recv,
):
    S, X, Y, Z = out.shape
    C = table.shape[1]
    NC = Y // ROWS
    NG = h0_send.shape[1]
    group_rows = Y // NG
    per_group = group_rows // ROWS
    tm = lax.axis_index("tm")
    sp = lax.axis_index("space")
    has_up = sp < SP - 1
    has_down = sp > 0
    has_next = tm < TM - 1
    has_prev = tm > 0

    def rows(c):
        return pl.ds(pl.multiple_of(c * ROWS, ROWS), ROWS)

    def padded_rows(c):
        return pl.ds(pl.multiple_of(c * ROWS + PAD, ROWS), ROWS)

    def remote(src, dst, send, recv, **device):
        return pltpu.make_async_remote_copy(
            src_ref=src, dst_ref=dst, send_sem=send, recv_sem=recv,
            device_id=device, device_id_type=pl.DeviceIdType.MESH,
        )

    def cls_copy(k):
        edge = X - 1 if k == 0 else 0
        place = 0 if k == 0 else X + 1
        to = sp + 1 if k == 0 else sp - 1
        return remote(classes.at[edge], cl.at[place], cls_send.at[k], cls_recv.at[k], space=to)

    def h0_copy(k, g):
        edge = X - 1 if k == 0 else 0
        place = 0 if k == 0 else X + 1
        to = sp + 1 if k == 0 else sp - 1
        src = starts.at[0, :, edge, pl.ds(pl.multiple_of(g * group_rows, ROWS), group_rows), :]
        dst = u0.at[:, place, pl.ds(pl.multiple_of(g * group_rows + PAD, ROWS), group_rows), :]
        return remote(src, dst, h0_send.at[k, g], h0_recv.at[k, g], space=to)

    def halo_copy(field, send, recv, k, c):
        edge = X if k == 0 else 1
        place = 0 if k == 0 else X + 1
        to = sp + 1 if k == 0 else sp - 1
        return remote(
            field.at[:, edge, padded_rows(c), :], field.at[:, place, padded_rows(c), :],
            send.at[k, c], recv.at[k, c], space=to,
        )

    h1_copy = functools.partial(halo_copy, u1, h1_send, h1_recv)
    wh_copy = functools.partial(halo_copy, w, wh_send, wh_recv)

    def w_copy(c):
        return remote(
            out.at[:, :, rows(c), :], w.at[:, pl.ds(1, X), padded_rows(c), :],
            w_send.at[c], w_recv.at[c], tm=tm + 1,
        )

    def start_both(copy, *args):
        pl.when(has_up)(lambda: copy(0, *args).start())
        pl.when(has_down)(lambda: copy(1, *args).start())

    def recv_both(copy, *args):
        pl.when(has_down)(lambda: copy(0, *args).wait_recv())
        pl.when(has_up)(lambda: copy(1, *args).wait_recv())

    def sent_both(copy, *args):
        pl.when(has_up)(lambda: copy(0, *args).wait_send())
        pl.when(has_down)(lambda: copy(1, *args).wait_send())

    start_in = pltpu.make_async_copy(
        starts.at[0], u0.at[:, pl.ds(1, X), pl.ds(PAD, Y), :], local_sem.at[0]
    )
    class_in = pltpu.make_async_copy(classes, cl.at[pl.ds(1, X)], local_sem.at[1])
    start_in.start()
    class_in.start()

    barrier = pltpu.get_barrier_semaphore()
    for exists, device in (
        (has_up, dict(space=sp + 1)), (has_down, dict(space=sp - 1)),
        (has_next, dict(tm=tm + 1)), (has_prev, dict(tm=tm - 1)),
    ):
        def greet(device=device):
            pl.semaphore_signal(
                barrier, inc=1, device_id=device, device_id_type=pl.DeviceIdType.MESH
            )
        pl.when(exists)(greet)

    tile_all = jnp.zeros((X + 2, PAD, Z), jnp.float32)

    def clear(s, carry):
        for field in (u0, u1, w):
            field[s, :, 0:PAD, :] = tile_all
            field[s, :, Y + PAD : Y + 2 * PAD, :] = tile_all
        outside = jnp.full((X + 2, PAD, Z), table[s, 0] * 0.125, jnp.float32)
        kq[s, :, 0:PAD, :] = outside
        kq[s, :, Y + PAD : Y + 2 * PAD, :] = outside
        return carry

    lax.fori_loop(0, S, clear, 0)

    def clear_plane(place):
        def one(s, carry):
            for field in (u0, u1, w):
                field[s, place, PAD : Y + PAD, :] = jnp.zeros((Y, Z), jnp.float32)
            return carry
        lax.fori_loop(0, S, one, 0, unroll=UNROLL)
        cl[place] = jnp.zeros((Y, Z), jnp.int32)

    pl.when(jnp.logical_not(has_down))(lambda: clear_plane(0))
    pl.when(jnp.logical_not(has_up))(lambda: clear_plane(X + 1))

    neighbours = (
        has_up.astype(jnp.int32) + has_down.astype(jnp.int32)
        + has_next.astype(jnp.int32) + has_prev.astype(jnp.int32)
    )
    pl.semaphore_wait(barrier, neighbours)

    start_both(cls_copy)
    for g in range(NG):
        start_both(h0_copy, g)
    start_in.wait()
    class_in.wait()
    recv_both(cls_copy)

    lane = lax.broadcasted_iota(jnp.int32, (X, ROWS, Z), 2)
    at_first = lane == 0
    at_last = lane == Z - 1

    def behind(value, fill=0.0):
        return jnp.where(at_first, fill, pltpu.roll(value, 1, 2))

    def ahead(value, fill=0.0):
        return jnp.where(at_last, fill, pltpu.roll(value, Z - 1, 2))

    def three(field, s, c, inner):
        base = c * ROWS + PAD
        planes = pl.ds(1, X) if inner else slice(None)
        before = field[s, planes, pl.ds(base - 1, ROWS), :]
        here = field[s, :, padded_rows(c), :]
        after = field[s, planes, pl.ds(base + 1, ROWS), :]
        return before, here, after

    def smooth_x(value):
        middle = value[1:-1]
        return (value[:-2] + value[2:]) + (middle + middle)

    def kappa(c):
        found = cl[:, rows(c), :]
        bits = []
        level = 1
        while level < C:
            bits.append((found & level) != 0)
            level *= 2

        def one(s, carry):
            values = [table[s, i] for i in range(C)]
            for bit in bits:
                values = [
                    jnp.where(bit, values[i + 1], values[i]) if i + 1 < len(values) else values[i]
                    for i in range(0, len(values), 2)
                ]
            kq[s, :, padded_rows(c), :] = jnp.broadcast_to(values[0], found.shape) * 0.125
            return carry

        lax.fori_loop(0, S, one, 0, unroll=UNROLL)

    def coefficients(c):
        def one(s, carry):
            before, here, after = three(kq, s, c, False)
            outside = table[s, 0] * 0.125
            mid = here[1:-1]
            smooth = smooth_x((before + after) + (here + here))
            smooth = (smooth + smooth) + (
                behind(smooth, outside * 16.0) + ahead(smooth, outside * 16.0)
            )
            ef[s, :, rows(c), :] = (1.0 - sum(fine_courant)) - 64.0 * mid - smooth
            faces = (here[:-2] + here[2:]) + (before[1:-1] + after[1:-1])
            faces = faces + (behind(mid, outside) + ahead(mid, outside))
            ec[s, :, rows(c), :] = (1.0 - sum(coarse_courant)) - 96.0 * mid - 16.0 * faces
            return carry

        lax.fori_loop(0, S, one, 0, unroll=UNROLL)

    def fine_move(field, s, c):
        before, here, after = three(field, s, c, False)
        k_before, k_here, k_after = three(kq, s, c, False)
        product = k_here * here
        weighted = (k_before * before + k_after * after) + (product + product)
        plain = smooth_x((before + after) + (here + here))
        weighted = smooth_x(weighted)
        mid = here[1:-1]
        result = mid * ef[s, :, rows(c), :]
        result += fine_courant[0] * here[:-2] + fine_courant[1] * before[1:-1]
        result += k_here[1:-1] * ((plain + plain) + (behind(plain) + ahead(plain)))
        result += (weighted + weighted) + (
            behind(weighted + fine_courant[2] * mid) + ahead(weighted)
        )
        return result

    def coarse_move(field, s, c):
        before, here, after = three(field, s, c, True)
        k_before, k_here, k_after = three(kq, s, c, True)
        mid = here[1:-1]
        k_mid = k_here[1:-1]
        product = k_here * here
        mid_product = product[1:-1]
        plain = (here[:-2] + here[2:]) + (before + after)
        plain = plain + (behind(mid) + ahead(mid))
        weighted = (product[:-2] + product[2:]) + (k_before * before + k_after * after)
        weighted = weighted + (
            behind(mid_product + (coarse_courant[2] / 16.0) * mid) + ahead(mid_product)
        )
        result = mid * ec[s, :, rows(c), :]
        result += coarse_courant[0] * here[:-2] + coarse_courant[1] * before
        return result + 16.0 * (k_mid * plain + weighted)

    def mix(store):
        values = [moved[t] for t in range(S)]
        for s in range(S):
            total = mixing[s, 0] * values[0]
            for t in range(1, S):
                total += mixing[s, t] * values[t]
            store(s, total)

    def each_species(move):
        def one(s, carry):
            moved[s] = move(s)
            return carry
        lax.fori_loop(0, S, one, 0, unroll=UNROLL)

    def first_fine(c):
        each_species(lambda s: fine_move(u0, s, c))

        def store(s, value):
            u1[s, 1 : X + 1, padded_rows(c), :] = value

        mix(store)
        start_both(h1_copy, c)

    def store_out(c):
        def store(s, value):
            out[s, :, rows(c), :] = value
        return store

    def second_fine(c):
        @pl.when(jnp.logical_not(has_prev))
        def _():
            each_species(lambda s: fine_move(u1, s, c))
            mix(store_out(c))
            pl.when(has_next)(lambda: w_copy(c).start())

        @pl.when(has_prev)
        def _():
            each_species(lambda s: fine_move(u1, s, c) - coarse_move(u0, s, c))
            mix(store_out(c))

    def own_step(t):
        @pl.when(t < NC)
        def _():
            pl.when(lax.rem(t, per_group) == 0)(lambda: recv_both(h0_copy, t // per_group))
            kappa(t)

        @pl.when(jnp.logical_and(t >= 1, t <= NC))
        def _():
            coefficients(t - 1)
            first_fine(t - 1)

        @pl.when(jnp.logical_and(t >= BEHIND - 1, t <= NC + BEHIND - 2))
        def _():
            recv_both(h1_copy, t - (BEHIND - 1))

        pl.when(jnp.logical_and(t >= BEHIND, t < NC + BEHIND))(lambda: second_fine(t - BEHIND))

    def chain_step(t):
        @pl.when(t < NC)
        def _():
            w_copy(t).wait_recv()
            start_both(wh_copy, t)

        @pl.when(t >= 1)
        def _():
            c = t - 1
            recv_both(wh_copy, c)
            each_species(lambda s: coarse_move(w, s, c))

            def store(s, value):
                out[s, :, rows(c), :] = out[s, :, rows(c), :] + value

            mix(store)
            pl.when(has_next)(lambda: w_copy(c).start())

    chain_from = BEHIND + LAG * tm + LAG0

    def step(t, carry):
        chain_t = t - chain_from
        pl.when(jnp.logical_and(has_prev, jnp.logical_and(chain_t >= 0, chain_t <= NC)))(
            lambda: chain_step(chain_t)
        )
        pl.when(t < NC + BEHIND)(lambda: own_step(t))
        return carry

    steps = jnp.where(has_prev, chain_from + NC + 1, NC + BEHIND)
    lax.fori_loop(0, steps, step, 0)

    sent_both(cls_copy)
    for g in range(NG):
        sent_both(h0_copy, g)

    def finish(c, carry):
        sent_both(h1_copy, c)
        pl.when(has_prev)(lambda: sent_both(wh_copy, c))
        pl.when(has_next)(lambda: w_copy(c).wait_send())
        return carry

    lax.fori_loop(0, NC, finish, 0)


def solution(mesh):
    TM, SP = mesh.shape["tm"], mesh.shape["space"]

    def body(starts, classes, table, mixing):
        _, S, X, Y, Z = starts.shape
        NC = Y // ROWS
        NG = 4
        padded = pltpu.VMEM((S, X + 2, Y + 2 * PAD, Z), jnp.float32)
        plain = pltpu.VMEM((S, X, Y, Z), jnp.float32)
        dma = pltpu.SemaphoreType.DMA
        result = pl.pallas_call(
            functools.partial(kernel, TM, SP),
            out_shape=jax.ShapeDtypeStruct((S, X, Y, Z), jnp.float32),
            in_specs=[
                pl.BlockSpec(memory_space=pltpu.SMEM),
                pl.BlockSpec(memory_space=pltpu.SMEM),
                pl.BlockSpec(memory_space=pl.ANY),
                pl.BlockSpec(memory_space=pl.ANY),
            ],
            out_specs=pl.BlockSpec(memory_space=pltpu.VMEM),
            scratch_shapes=[
                padded, padded, padded, padded, plain, plain,
                pltpu.VMEM((X + 2, Y, Z), jnp.int32),
                pltpu.VMEM((S, X, ROWS, Z), jnp.float32),
                dma((2,)), dma((2,)), dma((2,)), dma((2, NG)), dma((2, NG)),
                dma((2, NC)), dma((2, NC)), dma((2, NC)), dma((2, NC)),
                dma((NC,)), dma((NC,)),
            ],
            compiler_params=pltpu.CompilerParams(
                collective_id=0, has_side_effects=True, vmem_limit_bytes=48 * 1024 * 1024
            ),
        )(table.T, mixing, starts, classes)
        return result[None]

    in_specs = (P("tm", None, "space", None, None), P("space", None, None), P(), P())
    out_specs = P("tm", None, "space", None, None)
    return jax.shard_map(body, mesh=mesh, in_specs=in_specs, out_specs=out_specs, check_vma=False)
```

```python
import functools

import jax
import jax.numpy as jnp
from jax import lax
from jax.experimental import pallas as pl
from jax.experimental.pallas import tpu as pltpu
from jax.sharding import PartitionSpec as P

ROWS = 8
BEHIND = 4
LAG = 2
LAG0 = 0
UNROLL = 8
PAD = 8
fine_courant = (0.15, 0.1, 0.05)
coarse_courant = (0.3, 0.2, 0.1)


def kernel(
    TM, SP, table_in, mixing_in, starts, classes, out,
    table, mixing, u0, u1, w, kq, ef, ec, cl, moved,
    local_sem, cls_send, cls_recv, h0_send, h0_recv, h1_send, h1_recv,
    wh_send, wh_recv, w_send, w_recv,
):
    S, X, Y, Z = out.shape
    C = table.shape[1]
    NC = Y // ROWS
    NG = h0_send.shape[1]
    group_rows = Y // NG
    per_group = group_rows // ROWS
    tm = lax.axis_index("tm")
    sp = lax.axis_index("space")
    has_up = sp < SP - 1
    has_down = sp > 0
    has_next = tm < TM - 1
    has_prev = tm > 0

    def rows(c):
        return pl.ds(pl.multiple_of(c * ROWS, ROWS), ROWS)

    def padded_rows(c):
        return pl.ds(pl.multiple_of(c * ROWS + PAD, ROWS), ROWS)

    def remote(src, dst, send, recv, **device):
        return pltpu.make_async_remote_copy(
            src_ref=src, dst_ref=dst, send_sem=send, recv_sem=recv,
            device_id=device, device_id_type=pl.DeviceIdType.MESH,
        )

    def cls_copy(k):
        edge = X - 1 if k == 0 else 0
        place = 0 if k == 0 else X + 1
        to = sp + 1 if k == 0 else sp - 1
        return remote(classes.at[edge], cl.at[place], cls_send.at[k], cls_recv.at[k], space=to)

    def h0_copy(k, g):
        edge = X - 1 if k == 0 else 0
        place = 0 if k == 0 else X + 1
        to = sp + 1 if k == 0 else sp - 1
        src = starts.at[0, :, edge, pl.ds(pl.multiple_of(g * group_rows, ROWS), group_rows), :]
        dst = u0.at[:, place, pl.ds(pl.multiple_of(g * group_rows + PAD, ROWS), group_rows), :]
        return remote(src, dst, h0_send.at[k, g], h0_recv.at[k, g], space=to)

    def halo_copy(field, send, recv, k, c):
        edge = X if k == 0 else 1
        place = 0 if k == 0 else X + 1
        to = sp + 1 if k == 0 else sp - 1
        return remote(
            field.at[:, edge, padded_rows(c), :], field.at[:, place, padded_rows(c), :],
            send.at[k, c], recv.at[k, c], space=to,
        )

    h1_copy = functools.partial(halo_copy, u1, h1_send, h1_recv)
    wh_copy = functools.partial(halo_copy, w, wh_send, wh_recv)

    def w_copy(c):
        return remote(
            out.at[:, :, rows(c), :], w.at[:, pl.ds(1, X), padded_rows(c), :],
            w_send.at[c], w_recv.at[c], tm=tm + 1,
        )

    def start_both(copy, *args):
        pl.when(has_up)(lambda: copy(0, *args).start())
        pl.when(has_down)(lambda: copy(1, *args).start())

    def recv_both(copy, *args):
        pl.when(has_down)(lambda: copy(0, *args).wait_recv())
        pl.when(has_up)(lambda: copy(1, *args).wait_recv())

    def sent_both(copy, *args):
        pl.when(has_up)(lambda: copy(0, *args).wait_send())
        pl.when(has_down)(lambda: copy(1, *args).wait_send())

    start_in = pltpu.make_async_copy(
        starts.at[0], u0.at[:, pl.ds(1, X), pl.ds(PAD, Y), :], local_sem.at[0]
    )
    class_in = pltpu.make_async_copy(classes, cl.at[pl.ds(1, X)], local_sem.at[1])
    table_copy = pltpu.make_async_copy(table_in, table, local_sem.at[2])
    mixing_copy = pltpu.make_async_copy(mixing_in, mixing, local_sem.at[3])
    table_copy.start()
    class_in.start()
    start_in.start()
    mixing_copy.start()

    barrier = pltpu.get_barrier_semaphore()
    for exists, device in (
        (has_up, dict(space=sp + 1)), (has_down, dict(space=sp - 1)),
        (has_next, dict(tm=tm + 1)), (has_prev, dict(tm=tm - 1)),
    ):
        def greet(device=device):
            pl.semaphore_signal(
                barrier, inc=1, device_id=device, device_id_type=pl.DeviceIdType.MESH
            )
        pl.when(exists)(greet)

    tile_all = jnp.zeros((X + 2, PAD, Z), jnp.float32)

    def clear(s, carry):
        for field in (u0, u1, w):
            field[s, :, 0:PAD, :] = tile_all
            field[s, :, Y + PAD : Y + 2 * PAD, :] = tile_all
        return carry

    def outside_rows(s, carry):
        outside = jnp.full((X + 2, PAD, Z), table[s, 0] * 0.125, jnp.float32)
        kq[s, :, 0:PAD, :] = outside
        kq[s, :, Y + PAD : Y + 2 * PAD, :] = outside
        return carry

    lax.fori_loop(0, S, clear, 0)


    def clear_plane(place):
        def one(s, carry):
            for field in (u0, u1, w):
                field[s, place, PAD : Y + PAD, :] = jnp.zeros((Y, Z), jnp.float32)
            return carry
        lax.fori_loop(0, S, one, 0, unroll=UNROLL)
        cl[place] = jnp.zeros((Y, Z), jnp.int32)

    pl.when(jnp.logical_not(has_down))(lambda: clear_plane(0))
    pl.when(jnp.logical_not(has_up))(lambda: clear_plane(X + 1))

    neighbours = (
        has_up.astype(jnp.int32) + has_down.astype(jnp.int32)
        + has_next.astype(jnp.int32) + has_prev.astype(jnp.int32)
    )
    pl.semaphore_wait(barrier, neighbours)

    start_both(cls_copy)
    for g in range(NG):
        start_both(h0_copy, g)
    table_copy.wait()
    lax.fori_loop(0, S, outside_rows, 0)
    mixing_copy.wait()
    start_in.wait()
    class_in.wait()
    recv_both(cls_copy)

    lane = lax.broadcasted_iota(jnp.int32, (X, ROWS, Z), 2)
    at_first = lane == 0
    at_last = lane == Z - 1

    def behind(value, fill=0.0):
        return jnp.where(at_first, fill, pltpu.roll(value, 1, 2))

    def ahead(value, fill=0.0):
        return jnp.where(at_last, fill, pltpu.roll(value, Z - 1, 2))

    def three(field, s, c, inner):
        base = c * ROWS + PAD
        planes = pl.ds(1, X) if inner else slice(None)
        before = field[s, planes, pl.ds(base - 1, ROWS), :]
        here = field[s, :, padded_rows(c), :]
        after = field[s, planes, pl.ds(base + 1, ROWS), :]
        return before, here, after

    def smooth_x(value):
        middle = value[1:-1]
        return (value[:-2] + value[2:]) + (middle + middle)

    def kappa(c):
        found = cl[:, rows(c), :]
        bits = []
        level = 1
        while level < C:
            bits.append((found & level) != 0)
            level *= 2

        def one(s, carry):
            values = [table[s, i] for i in range(C)]
            for bit in bits:
                values = [
                    jnp.where(bit, values[i + 1], values[i]) if i + 1 < len(values) else values[i]
                    for i in range(0, len(values), 2)
                ]
            kq[s, :, padded_rows(c), :] = jnp.broadcast_to(values[0], found.shape) * 0.125
            return carry

        lax.fori_loop(0, S, one, 0, unroll=UNROLL)

    def coefficients(c, with_coarse):
        def one(s, carry):
            before, here, after = three(kq, s, c, False)
            outside = table[s, 0] * 0.125
            mid = here[1:-1]
            smooth = smooth_x((before + after) + (here + here))
            smooth = (smooth + smooth) + (
                behind(smooth, outside * 16.0) + ahead(smooth, outside * 16.0)
            )
            ef[s, :, rows(c), :] = (1.0 - sum(fine_courant)) - 64.0 * mid - smooth
            if not with_coarse:
                return carry
            faces = (here[:-2] + here[2:]) + (before[1:-1] + after[1:-1])
            faces = faces + (behind(mid, outside) + ahead(mid, outside))
            ec[s, :, rows(c), :] = (1.0 - sum(coarse_courant)) - 96.0 * mid - 16.0 * faces
            return carry

        lax.fori_loop(0, S, one, 0, unroll=UNROLL)

    def fine_move(field, s, c):
        before, here, after = three(field, s, c, False)
        k_before, k_here, k_after = three(kq, s, c, False)
        product = k_here * here
        weighted = (k_before * before + k_after * after) + (product + product)
        plain = smooth_x((before + after) + (here + here))
        weighted = smooth_x(weighted)
        mid = here[1:-1]
        result = mid * ef[s, :, rows(c), :]
        result += fine_courant[0] * here[:-2] + fine_courant[1] * before[1:-1]
        result += k_here[1:-1] * ((plain + plain) + (behind(plain) + ahead(plain)))
        result += (weighted + weighted) + (
            behind(weighted + fine_courant[2] * mid) + ahead(weighted)
        )
        return result

    def coarse_move(field, s, c):
        before, here, after = three(field, s, c, True)
        k_before, k_here, k_after = three(kq, s, c, True)
        mid = here[1:-1]
        k_mid = k_here[1:-1]
        product = k_here * here
        mid_product = product[1:-1]
        plain = (here[:-2] + here[2:]) + (before + after)
        plain = plain + (behind(mid) + ahead(mid))
        weighted = (product[:-2] + product[2:]) + (k_before * before + k_after * after)
        weighted = weighted + (
            behind(mid_product + (coarse_courant[2] / 16.0) * mid) + ahead(mid_product)
        )
        result = mid * ec[s, :, rows(c), :]
        result += coarse_courant[0] * here[:-2] + coarse_courant[1] * before
        return result + 16.0 * (k_mid * plain + weighted)

    def mix(store):
        values = [moved[t] for t in range(S)]
        for s in range(S):
            total = mixing[s, 0] * values[0]
            for t in range(1, S):
                total += mixing[s, t] * values[t]
            store(s, total)

    def each_species(move):
        def one(s, carry):
            moved[s] = move(s)
            return carry
        lax.fori_loop(0, S, one, 0, unroll=UNROLL)

    def first_fine(c):
        each_species(lambda s: fine_move(u0, s, c))

        def store(s, value):
            u1[s, 1 : X + 1, padded_rows(c), :] = value

        mix(store)
        start_both(h1_copy, c)

    def store_out(c):
        def store(s, value):
            out[s, :, rows(c), :] = value
        return store

    def second_fine(c):
        @pl.when(jnp.logical_not(has_prev))
        def _():
            each_species(lambda s: fine_move(u1, s, c))
            mix(store_out(c))
            pl.when(has_next)(lambda: w_copy(c).start())

        @pl.when(has_prev)
        def _():
            each_species(lambda s: fine_move(u1, s, c) - coarse_move(u0, s, c))
            mix(store_out(c))

    def own_step(t):
        @pl.when(t < NC)
        def _():
            pl.when(lax.rem(t, per_group) == 0)(lambda: recv_both(h0_copy, t // per_group))
            kappa(t)

        @pl.when(jnp.logical_and(t >= 1, t <= NC))
        def _():
            pl.when(has_prev)(lambda: coefficients(t - 1, True))
            pl.when(jnp.logical_not(has_prev))(lambda: coefficients(t - 1, False))
            first_fine(t - 1)

        @pl.when(jnp.logical_and(t >= BEHIND - 1, t <= NC + BEHIND - 2))
        def _():
            recv_both(h1_copy, t - (BEHIND - 1))

        pl.when(jnp.logical_and(t >= BEHIND, t < NC + BEHIND))(lambda: second_fine(t - BEHIND))

    def chain_step(t):
        @pl.when(t < NC)
        def _():
            w_copy(t).wait_recv()
            start_both(wh_copy, t)

        @pl.when(t >= 1)
        def _():
            c = t - 1
            recv_both(wh_copy, c)
            each_species(lambda s: coarse_move(w, s, c))

            def store(s, value):
                out[s, :, rows(c), :] = out[s, :, rows(c), :] + value

            mix(store)
            pl.when(has_next)(lambda: w_copy(c).start())

    chain_from = BEHIND + LAG * tm + LAG0

    def step(t, carry):
        chain_t = t - chain_from
        pl.when(jnp.logical_and(has_prev, jnp.logical_and(chain_t >= 0, chain_t <= NC)))(
            lambda: chain_step(chain_t)
        )
        pl.when(t < NC + BEHIND)(lambda: own_step(t))
        return carry

    steps = jnp.where(has_prev, chain_from + NC + 1, NC + BEHIND)
    lax.fori_loop(0, steps, step, 0)

    sent_both(cls_copy)
    for g in range(NG):
        sent_both(h0_copy, g)

    def finish(c, carry):
        sent_both(h1_copy, c)
        pl.when(has_prev)(lambda: sent_both(wh_copy, c))
        pl.when(has_next)(lambda: w_copy(c).wait_send())
        return carry

    lax.fori_loop(0, NC, finish, 0)


def solution(mesh):
    TM, SP = mesh.shape["tm"], mesh.shape["space"]

    def body(starts, classes, table, mixing):
        _, S, X, Y, Z = starts.shape
        NC = Y // ROWS
        NG = 4
        padded = pltpu.VMEM((S, X + 2, Y + 2 * PAD, Z), jnp.float32)
        plain = pltpu.VMEM((S, X, Y, Z), jnp.float32)
        dma = pltpu.SemaphoreType.DMA
        result = pl.pallas_call(
            functools.partial(kernel, TM, SP),
            out_shape=jax.ShapeDtypeStruct((S, X, Y, Z), jnp.float32),
            in_specs=[
                pl.BlockSpec(memory_space=pltpu.HBM),
                pl.BlockSpec(memory_space=pltpu.HBM),
                pl.BlockSpec(memory_space=pltpu.HBM),
                pl.BlockSpec(memory_space=pltpu.HBM),
            ],
            out_specs=pl.BlockSpec(memory_space=pltpu.VMEM),
            scratch_shapes=[
                pltpu.SMEM(table.shape[::-1], jnp.float32),
                pltpu.SMEM(mixing.shape, jnp.float32),
                padded, padded, padded, padded, plain, plain,
                pltpu.VMEM((X + 2, Y, Z), jnp.int32),
                pltpu.VMEM((S, X, ROWS, Z), jnp.float32),
                dma((4,)), dma((2,)), dma((2,)), dma((2, NG)), dma((2, NG)),
                dma((2, NC)), dma((2, NC)), dma((2, NC)), dma((2, NC)),
                dma((NC,)), dma((NC,)),
            ],
            compiler_params=pltpu.CompilerParams(
                collective_id=0, has_side_effects=True, vmem_limit_bytes=62 * 1024 * 1024
            ),
        )(table.T, mixing, starts, classes)
        return result[None]

    in_specs = (P("tm", None, "space", None, None), P("space", None, None), P(), P())
    out_specs = P("tm", None, "space", None, None)
    return jax.shard_map(body, mesh=mesh, in_specs=in_specs, out_specs=out_specs, check_vma=False)
```

```python
import functools

import jax
import jax.numpy as jnp
from jax import lax
from jax.experimental import pallas as pl
from jax.experimental.pallas import tpu as pltpu
from jax.sharding import PartitionSpec as P

ROWS = 8
BEHIND = 4
LAG = 2
LAG0 = 0
UNROLL = 8
PAD = 8
fine_courant = (0.15, 0.1, 0.05)
coarse_courant = (0.3, 0.2, 0.1)


def kernel(
    TM, SP, table_in, mixing_in, starts, classes, out_far,
    out, out_sem, table, mixing, u0, u1, w, kq, ef, ec, cl, moved,
    local_sem, cls_send, cls_recv, h0_send, h0_recv, h1_send, h1_recv,
    wh_send, wh_recv, w_send, w_recv,
):
    S, X, Y, Z = out.shape
    C = table.shape[1]
    NC = Y // ROWS
    NG = h0_send.shape[1]
    group_rows = Y // NG
    per_group = group_rows // ROWS
    tm = lax.axis_index("tm")
    sp = lax.axis_index("space")
    has_up = sp < SP - 1
    has_down = sp > 0
    has_next = tm < TM - 1
    has_prev = tm > 0

    def rows(c):
        return pl.ds(pl.multiple_of(c * ROWS, ROWS), ROWS)

    def padded_rows(c):
        return pl.ds(pl.multiple_of(c * ROWS + PAD, ROWS), ROWS)

    def remote(src, dst, send, recv, **device):
        return pltpu.make_async_remote_copy(
            src_ref=src, dst_ref=dst, send_sem=send, recv_sem=recv,
            device_id=device, device_id_type=pl.DeviceIdType.MESH,
        )

    def cls_copy(k):
        edge = X - 1 if k == 0 else 0
        place = 0 if k == 0 else X + 1
        to = sp + 1 if k == 0 else sp - 1
        return remote(classes.at[edge], cl.at[place], cls_send.at[k], cls_recv.at[k], space=to)

    def h0_copy(k, g):
        edge = X - 1 if k == 0 else 0
        place = 0 if k == 0 else X + 1
        to = sp + 1 if k == 0 else sp - 1
        src = starts.at[0, :, edge, pl.ds(pl.multiple_of(g * group_rows, ROWS), group_rows), :]
        dst = u0.at[:, place, pl.ds(pl.multiple_of(g * group_rows + PAD, ROWS), group_rows), :]
        return remote(src, dst, h0_send.at[k, g], h0_recv.at[k, g], space=to)

    def halo_copy(field, send, recv, k, c):
        edge = X if k == 0 else 1
        place = 0 if k == 0 else X + 1
        to = sp + 1 if k == 0 else sp - 1
        return remote(
            field.at[:, edge, padded_rows(c), :], field.at[:, place, padded_rows(c), :],
            send.at[k, c], recv.at[k, c], space=to,
        )

    h1_copy = functools.partial(halo_copy, u1, h1_send, h1_recv)
    wh_copy = functools.partial(halo_copy, w, wh_send, wh_recv)

    def w_copy(c):
        return remote(
            out.at[:, :, rows(c), :], w.at[:, pl.ds(1, X), padded_rows(c), :],
            w_send.at[c], w_recv.at[c], tm=tm + 1,
        )

    def out_copy(c):
        return pltpu.make_async_copy(
            out.at[:, :, rows(c), :], out_far.at[:, :, rows(c), :], out_sem.at[c]
        )

    def start_both(copy, *args):
        pl.when(has_up)(lambda: copy(0, *args).start())
        pl.when(has_down)(lambda: copy(1, *args).start())

    def recv_both(copy, *args):
        pl.when(has_down)(lambda: copy(0, *args).wait_recv())
        pl.when(has_up)(lambda: copy(1, *args).wait_recv())

    def sent_both(copy, *args):
        pl.when(has_up)(lambda: copy(0, *args).wait_send())
        pl.when(has_down)(lambda: copy(1, *args).wait_send())

    start_in = pltpu.make_async_copy(
        starts.at[0], u0.at[:, pl.ds(1, X), pl.ds(PAD, Y), :], local_sem.at[0]
    )
    class_in = pltpu.make_async_copy(classes, cl.at[pl.ds(1, X)], local_sem.at[1])
    table_copy = pltpu.make_async_copy(table_in, table, local_sem.at[2])
    mixing_copy = pltpu.make_async_copy(mixing_in, mixing, local_sem.at[3])
    table_copy.start()
    class_in.start()
    start_in.start()
    mixing_copy.start()

    barrier = pltpu.get_barrier_semaphore()
    for exists, device in (
        (has_up, dict(space=sp + 1)), (has_down, dict(space=sp - 1)),
        (has_next, dict(tm=tm + 1)), (has_prev, dict(tm=tm - 1)),
    ):
        def greet(device=device):
            pl.semaphore_signal(
                barrier, inc=1, device_id=device, device_id_type=pl.DeviceIdType.MESH
            )
        pl.when(exists)(greet)

    tile_all = jnp.zeros((X + 2, PAD, Z), jnp.float32)

    def clear(s, carry):
        for field in (u0, u1, w):
            field[s, :, 0:PAD, :] = tile_all
            field[s, :, Y + PAD : Y + 2 * PAD, :] = tile_all
        return carry

    def outside_rows(s, carry):
        outside = jnp.full((X + 2, PAD, Z), table[s, 0] * 0.125, jnp.float32)
        kq[s, :, 0:PAD, :] = outside
        kq[s, :, Y + PAD : Y + 2 * PAD, :] = outside
        return carry

    lax.fori_loop(0, S, clear, 0)


    def clear_plane(place):
        def one(s, carry):
            for field in (u0, u1, w):
                field[s, place, PAD : Y + PAD, :] = jnp.zeros((Y, Z), jnp.float32)
            return carry
        lax.fori_loop(0, S, one, 0, unroll=UNROLL)
        cl[place] = jnp.zeros((Y, Z), jnp.int32)

    pl.when(jnp.logical_not(has_down))(lambda: clear_plane(0))
    pl.when(jnp.logical_not(has_up))(lambda: clear_plane(X + 1))

    neighbours = (
        has_up.astype(jnp.int32) + has_down.astype(jnp.int32)
        + has_next.astype(jnp.int32) + has_prev.astype(jnp.int32)
    )
    pl.semaphore_wait(barrier, neighbours)

    start_both(cls_copy)
    for g in range(NG):
        start_both(h0_copy, g)
    table_copy.wait()
    lax.fori_loop(0, S, outside_rows, 0)
    mixing_copy.wait()
    start_in.wait()
    class_in.wait()
    recv_both(cls_copy)

    lane = lax.broadcasted_iota(jnp.int32, (X, ROWS, Z), 2)
    at_first = lane == 0
    at_last = lane == Z - 1

    def behind(value, fill=0.0):
        return jnp.where(at_first, fill, pltpu.roll(value, 1, 2))

    def ahead(value, fill=0.0):
        return jnp.where(at_last, fill, pltpu.roll(value, Z - 1, 2))

    def three(field, s, c, inner):
        base = c * ROWS + PAD
        planes = pl.ds(1, X) if inner else slice(None)
        before = field[s, planes, pl.ds(base - 1, ROWS), :]
        here = field[s, :, padded_rows(c), :]
        after = field[s, planes, pl.ds(base + 1, ROWS), :]
        return before, here, after

    def smooth_x(value):
        middle = value[1:-1]
        return (value[:-2] + value[2:]) + (middle + middle)

    def kappa(c):
        found = cl[:, rows(c), :]
        bits = []
        level = 1
        while level < C:
            bits.append((found & level) != 0)
            level *= 2

        def one(s, carry):
            values = [table[s, i] for i in range(C)]
            for bit in bits:
                values = [
                    jnp.where(bit, values[i + 1], values[i]) if i + 1 < len(values) else values[i]
                    for i in range(0, len(values), 2)
                ]
            kq[s, :, padded_rows(c), :] = jnp.broadcast_to(values[0], found.shape) * 0.125
            return carry

        lax.fori_loop(0, S, one, 0, unroll=UNROLL)

    def coefficients(c, with_coarse):
        def one(s, carry):
            before, here, after = three(kq, s, c, False)
            outside = table[s, 0] * 0.125
            mid = here[1:-1]
            smooth = smooth_x((before + after) + (here + here))
            smooth = (smooth + smooth) + (
                behind(smooth, outside * 16.0) + ahead(smooth, outside * 16.0)
            )
            ef[s, :, rows(c), :] = (1.0 - sum(fine_courant)) - 64.0 * mid - smooth
            if not with_coarse:
                return carry
            faces = (here[:-2] + here[2:]) + (before[1:-1] + after[1:-1])
            faces = faces + (behind(mid, outside) + ahead(mid, outside))
            ec[s, :, rows(c), :] = (1.0 - sum(coarse_courant)) - 96.0 * mid - 16.0 * faces
            return carry

        lax.fori_loop(0, S, one, 0, unroll=UNROLL)

    def fine_move(field, s, c):
        before, here, after = three(field, s, c, False)
        k_before, k_here, k_after = three(kq, s, c, False)
        product = k_here * here
        weighted = (k_before * before + k_after * after) + (product + product)
        plain = smooth_x((before + after) + (here + here))
        weighted = smooth_x(weighted)
        mid = here[1:-1]
        result = mid * ef[s, :, rows(c), :]
        result += fine_courant[0] * here[:-2] + fine_courant[1] * before[1:-1]
        result += k_here[1:-1] * ((plain + plain) + (behind(plain) + ahead(plain)))
        result += (weighted + weighted) + (
            behind(weighted + fine_courant[2] * mid) + ahead(weighted)
        )
        return result

    def coarse_move(field, s, c):
        before, here, after = three(field, s, c, True)
        k_before, k_here, k_after = three(kq, s, c, True)
        mid = here[1:-1]
        k_mid = k_here[1:-1]
        product = k_here * here
        mid_product = product[1:-1]
        plain = (here[:-2] + here[2:]) + (before + after)
        plain = plain + (behind(mid) + ahead(mid))
        weighted = (product[:-2] + product[2:]) + (k_before * before + k_after * after)
        weighted = weighted + (
            behind(mid_product + (coarse_courant[2] / 16.0) * mid) + ahead(mid_product)
        )
        result = mid * ec[s, :, rows(c), :]
        result += coarse_courant[0] * here[:-2] + coarse_courant[1] * before
        return result + 16.0 * (k_mid * plain + weighted)

    def mix(store):
        values = [moved[t] for t in range(S)]
        for s in range(S):
            total = mixing[s, 0] * values[0]
            for t in range(1, S):
                total += mixing[s, t] * values[t]
            store(s, total)

    def each_species(move):
        def one(s, carry):
            moved[s] = move(s)
            return carry
        lax.fori_loop(0, S, one, 0, unroll=UNROLL)

    def first_fine(c):
        each_species(lambda s: fine_move(u0, s, c))

        def store(s, value):
            u1[s, 1 : X + 1, padded_rows(c), :] = value

        mix(store)
        start_both(h1_copy, c)

    def store_out(c):
        def store(s, value):
            out[s, :, rows(c), :] = value
        return store

    def second_fine(c):
        @pl.when(jnp.logical_not(has_prev))
        def _():
            each_species(lambda s: fine_move(u1, s, c))
            mix(store_out(c))
            pl.when(has_next)(lambda: w_copy(c).start())
            out_copy(c).start()

        @pl.when(has_prev)
        def _():
            each_species(lambda s: fine_move(u1, s, c) - coarse_move(u0, s, c))
            mix(store_out(c))

    def own_step(t):
        @pl.when(t < NC)
        def _():
            pl.when(lax.rem(t, per_group) == 0)(lambda: recv_both(h0_copy, t // per_group))
            kappa(t)

        @pl.when(jnp.logical_and(t >= 1, t <= NC))
        def _():
            pl.when(has_prev)(lambda: coefficients(t - 1, True))
            pl.when(jnp.logical_not(has_prev))(lambda: coefficients(t - 1, False))
            first_fine(t - 1)

        @pl.when(jnp.logical_and(t >= BEHIND - 1, t <= NC + BEHIND - 2))
        def _():
            recv_both(h1_copy, t - (BEHIND - 1))

        pl.when(jnp.logical_and(t >= BEHIND, t < NC + BEHIND))(lambda: second_fine(t - BEHIND))

    def chain_step(t):
        @pl.when(t < NC)
        def _():
            w_copy(t).wait_recv()
            start_both(wh_copy, t)

        @pl.when(t >= 1)
        def _():
            c = t - 1
            recv_both(wh_copy, c)
            each_species(lambda s: coarse_move(w, s, c))

            def store(s, value):
                out[s, :, rows(c), :] = out[s, :, rows(c), :] + value

            mix(store)
            pl.when(has_next)(lambda: w_copy(c).start())
            out_copy(c).start()

    chain_from = BEHIND + LAG * tm + LAG0

    def step(t, carry):
        chain_t = t - chain_from
        pl.when(jnp.logical_and(has_prev, jnp.logical_and(chain_t >= 0, chain_t <= NC)))(
            lambda: chain_step(chain_t)
        )
        pl.when(t < NC + BEHIND)(lambda: own_step(t))
        return carry

    steps = jnp.where(has_prev, chain_from + NC + 1, NC + BEHIND)
    lax.fori_loop(0, steps, step, 0)

    sent_both(cls_copy)
    for g in range(NG):
        sent_both(h0_copy, g)

    def finish(c, carry):
        sent_both(h1_copy, c)
        pl.when(has_prev)(lambda: sent_both(wh_copy, c))
        pl.when(has_next)(lambda: w_copy(c).wait_send())
        out_copy(c).wait()
        return carry

    lax.fori_loop(0, NC, finish, 0)


def solution(mesh):
    TM, SP = mesh.shape["tm"], mesh.shape["space"]

    def body(starts, classes, table, mixing):
        _, S, X, Y, Z = starts.shape
        NC = Y // ROWS
        NG = 4
        padded = pltpu.VMEM((S, X + 2, Y + 2 * PAD, Z), jnp.float32)
        plain = pltpu.VMEM((S, X, Y, Z), jnp.float32)
        dma = pltpu.SemaphoreType.DMA
        result = pl.pallas_call(
            functools.partial(kernel, TM, SP),
            out_shape=jax.ShapeDtypeStruct((S, X, Y, Z), jnp.float32),
            in_specs=[
                pl.BlockSpec(memory_space=pltpu.HBM),
                pl.BlockSpec(memory_space=pltpu.HBM),
                pl.BlockSpec(memory_space=pltpu.HBM),
                pl.BlockSpec(memory_space=pltpu.HBM),
            ],
            out_specs=pl.BlockSpec(memory_space=pltpu.HBM),
            scratch_shapes=[
                plain, dma((NC,)),
                pltpu.SMEM(table.shape[::-1], jnp.float32),
                pltpu.SMEM(mixing.shape, jnp.float32),
                padded, padded, padded, padded, plain, plain,
                pltpu.VMEM((X + 2, Y, Z), jnp.int32),
                pltpu.VMEM((S, X, ROWS, Z), jnp.float32),
                dma((4,)), dma((2,)), dma((2,)), dma((2, NG)), dma((2, NG)),
                dma((2, NC)), dma((2, NC)), dma((2, NC)), dma((2, NC)),
                dma((NC,)), dma((NC,)),
            ],
            compiler_params=pltpu.CompilerParams(
                collective_id=0, has_side_effects=True, vmem_limit_bytes=62 * 1024 * 1024
            ),
        )(table.T, mixing, starts, classes)
        return result[None]

    in_specs = (P("tm", None, "space", None, None), P("space", None, None), P(), P())
    out_specs = P("tm", None, "space", None, None)
    return jax.shard_map(body, mesh=mesh, in_specs=in_specs, out_specs=out_specs, check_vma=False)
```
